256 devices in a mesh: row: 64 (over x, z, core), col: 4 (over y).
Axes of the slice: x: 4, y: 4, z: 8, core: 2. Of those that a mesh axis runs over, the one named last changes fastest.
Arguments:
- h_blocks: bfloat16 [3072, 128, 128], P(('row', 'col')), may hold values from -0.125 to 0.125
- block_ids: int32 [256, 64], replicated, may hold values from 0 to 3071, as said below
- pattern: int32 [256, 8, 8], P(('row', 'col')), may hold values 0 or 1
- result_grad: bfloat16 [262144, 128], P(('row', 'col')), may hold values from -6 to 6
Outputs:
- grad_blocks: float32 [3072, 128, 128], P(('row', 'col'))
The draws below stay inside these ranges and needn't reach their ends.
Inputs may be any that keep to these rules, and one draw needn't show every extreme that they name: `block_ids`: submatrix s sits on device s (devices numbered over row, then col). Stored block i lies on device i // 12 in its local slot i % 12. Of the 64 blocks of one submatrix, exactly 16 lie on devices of each col index and at most 1 on any one device. Of all blocks that the submatrices of one row index take from devices of one col index, at most 1 lie on devices of any one row index. Both bounds are reached in every draw.
All inputs are finite; a program needn't handle non-finite values. No bound on the sum of `pattern` on one device may be relied on, other than what follows from the above.
Results may differ from the reference program's by a relative error of at most 0.0034.
Values may be sent and summed in bfloat16 or wider, within the bound.
No kernel may reach another device: no remote copies, remote signals or barrier semaphores. Data moves between devices by JAX's collectives and lax.ppermute only.
A program may use at most 128 MiB of HBM per device.

```python
import jax
import jax.numpy as jnp
from jax import lax

SIDE_BLOCKS = 8
BLOCK_ROWS = 128
STORED_DEV = 12
ROW_DEVS = 64
COL_DEVS = 4
SUBMATRICES = 256
SUB_ORDER = 1024
ALL_STORED = 3072
COL_ROOM = 16


def draw_block_ids(key, part):
    key = jax.random.fold_in(key, 11)
    key_cols, key_rows, key_slots = jax.random.split(key, 3)
    entries = SIDE_BLOCKS * SIDE_BLOCKS
    source_perm = jax.vmap(lambda sub_key: jax.random.permutation(sub_key, entries))(jax.random.split(key_cols, SUBMATRICES))
    dest_col = source_perm // COL_ROOM
    within = source_perm % COL_ROOM
    source = jnp.arange(SUBMATRICES, dtype=jnp.int32)
    source_row = source // COL_DEVS
    source_col = source % COL_DEVS
    position = source_col[:, None] * COL_ROOM + within
    row_perms = jax.vmap(lambda sub_key: jax.random.permutation(sub_key, ROW_DEVS))(jax.random.split(key_rows, ROW_DEVS * COL_DEVS))
    middle = source_row[:, None] * COL_DEVS + dest_col
    dest_row = row_perms[middle, position % ROW_DEVS]
    local_slot = jax.random.randint(key_slots, (SUBMATRICES, entries), 0, STORED_DEV)
    return ((dest_row * COL_DEVS + dest_col) * STORED_DEV + local_slot).astype(jnp.int32)


def plant(drawn, rng, low, largest):
    extent = drawn.shape
    place = [jax.random.randint(jax.random.fold_in(rng, axis), (), 0, extent[axis]) for axis in range(len(extent))]
    drawn = drawn.at[tuple(place)].set(low)
    longest = extent.index(max(extent))
    place[longest] = (place[longest] + 1) % extent[longest]
    return drawn.at[tuple(place)].set(largest)


def steps_of(key, dims, cuts, smallest, top_value):
    def one(dim, parts):
        draws = jax.random.uniform(jax.random.fold_in(jax.random.fold_in(key, 6), dim), (parts,), jnp.float32, smallest / len(cuts), top_value / len(cuts))
        return jnp.repeat(jnp.exp(draws), dims[dim] // parts).reshape((-1,) + (1,) * (len(dims) - dim - 1))

    loudness = one(*cuts[0])
    for cut in cuts[1:]:
        loudness = loudness * one(*cut)
    return loudness


def noise(key, shape, deviation, reach, shards=(), held_as=jnp.bfloat16):
    values = jax.random.normal(key, shape, jnp.float32) * deviation
    if len(shards) > 0:
        values = steps_of(key, shape, shards, -0.22, 0.18) * values
    return jnp.clip(values, min=-reach, max=reach).astype(held_as)


def setup_inputs(seed: int = 0) -> dict:
    splits = jax.random.split(jax.random.key(seed), 5)
    h_blocks = noise(splits[0], (ALL_STORED, BLOCK_ROWS, BLOCK_ROWS), (2 * SUB_ORDER) ** -0.5, 0.125, ((0, 256),))
    block_ids = draw_block_ids(jax.random.fold_in(splits[4], 71), 0)
    pattern = plant((jax.random.randint(splits[2], (SUBMATRICES, SIDE_BLOCKS, SIDE_BLOCKS), 0, 4) < 3).astype(jnp.int32), jax.random.fold_in(splits[2], 1), 0, 1)
    result_grad = noise(splits[3], (SUBMATRICES * SUB_ORDER, BLOCK_ROWS), 1.0, 6.0, ((0, 256),))
    return dict(h_blocks=h_blocks, block_ids=block_ids, pattern=pattern, result_grad=result_grad)


def multiply(former, latter):
    return jnp.dot(former.astype(jnp.float32), latter.astype(jnp.float32), preferred_element_type=jnp.float32)


def assemble(blocks):
    return blocks.reshape(SIDE_BLOCKS, SIDE_BLOCKS, BLOCK_ROWS, BLOCK_ROWS).transpose(0, 2, 1, 3).reshape(SUB_ORDER, SUB_ORDER)


def split_blocks(matrix):
    return matrix.reshape(SIDE_BLOCKS, BLOCK_ROWS, SIDE_BLOCKS, BLOCK_ROWS).transpose(0, 2, 1, 3).reshape(SIDE_BLOCKS * SIDE_BLOCKS, BLOCK_ROWS, BLOCK_ROWS)


def adjoint(initial, result_cot):
    square = multiply(initial, initial).astype(jnp.bfloat16)
    iterate = (1.5 * initial.astype(jnp.float32) - 0.5 * multiply(initial, square)).astype(jnp.bfloat16)
    lead_cols = iterate[:, :BLOCK_ROWS]
    pulled = multiply(iterate.T, result_cot).astype(jnp.bfloat16)
    lead_square = multiply(iterate, lead_cols).astype(jnp.bfloat16)
    crossed = multiply(jnp.concatenate([pulled, result_cot], axis=1), jnp.concatenate([lead_cols, lead_square], axis=1).T)
    nearby = multiply(iterate.T, pulled)
    head_part = 1.5 * result_cot.astype(jnp.float32) - 0.5 * nearby - 0.5 * crossed[:, :BLOCK_ROWS]
    cot_iterate = jnp.concatenate([head_part, -0.5 * crossed[:, BLOCK_ROWS:]], axis=1).astype(jnp.bfloat16)
    inner_part = multiply(initial.T, cot_iterate).astype(jnp.bfloat16)
    term_left = multiply(square.T, cot_iterate)
    term_middle = multiply(inner_part, initial.T)
    term_right = multiply(cot_iterate, square.T)
    return 1.5 * cot_iterate.astype(jnp.float32) - 0.5 * (term_left + term_middle + term_right)


def reference(h_blocks, block_ids, pattern, result_grad):
    cot_all = result_grad.reshape(SUBMATRICES, SUB_ORDER, BLOCK_ROWS)
    entries = SIDE_BLOCKS * SIDE_BLOCKS

    def accumulate(running, inputs):
        sub_ids, sub_pattern, sub_cot = inputs
        keep_flags = sub_pattern.reshape(entries, 1, 1)
        fetched = jnp.take(h_blocks, sub_ids, axis=0)
        initial = assemble(fetched * keep_flags.astype(jnp.bfloat16))
        cot_initial = adjoint(initial, sub_cot)
        pieces = split_blocks(cot_initial) * keep_flags.astype(jnp.float32)
        return running.at[sub_ids].add(pieces), None

    start_sum = jnp.zeros((ALL_STORED, BLOCK_ROWS, BLOCK_ROWS), jnp.float32)
    final_sum, unused = lax.scan(accumulate, start_sum, (block_ids, pattern, cot_all))
    return final_sum
```

```python
import jax
import jax.numpy as jnp
from jax import lax
from jax.sharding import PartitionSpec as P


def multiply(former, latter):
    return jnp.dot(former, latter, preferred_element_type=jnp.float32)


def left_transposed(former, latter):
    return lax.dot_general(
        former, latter, (((0,), (0,)), ((), ())), preferred_element_type=jnp.float32
    )


def right_transposed(former, latter):
    return lax.dot_general(
        former, latter, (((1,), (1,)), ((), ())), preferred_element_type=jnp.float32
    )


def assemble(blocks, block_edge, block_width):
    full_order = block_edge * block_width
    return (
        blocks.reshape(block_edge, block_edge, block_width, block_width)
        .transpose(0, 2, 1, 3)
        .reshape(full_order, full_order)
    )


def split_blocks(matrix, block_edge, block_width):
    return (
        matrix.reshape(block_edge, block_width, block_edge, block_width)
        .transpose(0, 2, 1, 3)
        .reshape(block_edge * block_edge, block_width, block_width)
    )


def adjoint(initial, result_cot):
    block_width = result_cot.shape[1]
    square = multiply(initial, initial).astype(jnp.bfloat16)
    iterate = (1.5 * initial.astype(jnp.float32) - 0.5 * multiply(initial, square)).astype(
        jnp.bfloat16
    )
    lead_cols = iterate[:, :block_width]
    pulled = left_transposed(iterate, result_cot).astype(jnp.bfloat16)
    lead_square = multiply(iterate, lead_cols).astype(jnp.bfloat16)
    crossed = right_transposed(
        jnp.concatenate([pulled, result_cot], axis=1),
        jnp.concatenate([lead_cols, lead_square], axis=1),
    )
    nearby = left_transposed(iterate, pulled)
    head_part = 1.5 * result_cot.astype(jnp.float32) - 0.5 * nearby - 0.5 * crossed[:, :block_width]
    cot_iterate = jnp.concatenate([head_part, -0.5 * crossed[:, block_width:]], axis=1).astype(
        jnp.bfloat16
    )
    inner_part = left_transposed(initial, cot_iterate).astype(jnp.bfloat16)
    term_left = left_transposed(square, cot_iterate)
    term_middle = right_transposed(inner_part, initial)
    term_right = right_transposed(cot_iterate, square)
    return 1.5 * cot_iterate.astype(jnp.float32) - 0.5 * (term_left + term_middle + term_right)


def shards(h_blocks, block_ids, pattern, result_grad):
    row_count = lax.axis_size("row")
    col_count = lax.axis_size("col")
    my_row = lax.axis_index("row")
    my_col = lax.axis_index("col")
    slot_count, block_width, _ = h_blocks.shape
    block_edge = pattern.shape[1]
    entries = block_ids.shape[1]
    room = entries // col_count
    owner = block_ids // slot_count
    slot = block_ids % slot_count
    mine = (owner == my_row * col_count + my_col).reshape(row_count, -1)
    slot_of_row = jnp.sum(jnp.where(mine, slot.reshape(row_count, -1), 0), axis=1)
    near = lax.dynamic_slice_in_dim(owner, my_row * col_count, col_count, 0)
    near_row = near // col_count
    near_col = near % col_count
    ranks = jnp.arange(room)
    taken = near_col == my_col
    place = jnp.cumsum(taken.astype(jnp.int32), axis=1) - 1
    picks = jnp.logical_and(taken[:, :, None], place[:, :, None] == ranks)
    row_at = jnp.sum(jnp.where(picks, near_row[:, :, None], 0), axis=1).reshape(-1)
    where_row = jnp.sum(
        jnp.where(
            row_at[None, :] == jnp.arange(row_count)[:, None], jnp.arange(entries)[None, :], 0
        ),
        axis=1,
    )
    my_cols = lax.dynamic_index_in_dim(near_col, my_col, 0, keepdims=False)
    on_col = my_cols[None, :] == jnp.arange(col_count)[:, None]
    rank = jnp.sum(jnp.where(on_col, jnp.cumsum(on_col.astype(jnp.int32), axis=1) - 1, 0), axis=0)
    spot = my_cols * room + rank
    entry_at = jnp.sum(
        jnp.where(spot[None, :] == jnp.arange(entries)[:, None], jnp.arange(entries)[None, :], 0),
        axis=1,
    )
    keep_flags = pattern.reshape(entries, 1, 1)

    def over(blocks, axis):
        return lax.all_to_all(blocks, axis, split_axis=0, concat_axis=0, tiled=True)

    arrived = over(jnp.take(h_blocks, slot_of_row, axis=0), "row")
    arrived = over(jnp.take(arrived, row_at, axis=0), "col")
    fetched = jnp.take(arrived, spot, axis=0)
    initial = assemble(fetched * keep_flags.astype(jnp.bfloat16), block_edge, block_width)
    cot_initial = adjoint(initial, result_grad)
    pieces = split_blocks(cot_initial, block_edge, block_width) * keep_flags.astype(jnp.float32)
    leaving = jnp.take(pieces.astype(jnp.bfloat16), entry_at, axis=0)
    leaving = jnp.take(over(leaving, "col"), where_row, axis=0)
    landed = over(leaving, "row")
    weights = (slot_of_row[None, :] == jnp.arange(slot_count)[:, None]).astype(jnp.bfloat16)
    return jnp.einsum("sr,rab->sab", weights, landed, preferred_element_type=jnp.float32)


def solution(mesh):
    in_specs = (
        P(("row", "col"), None, None),
        P(),
        P(("row", "col"), None, None),
        P(("row", "col"), None),
    )
    out_specs = P(("row", "col"), None, None)
    return jax.shard_map(shards, mesh=mesh, in_specs=in_specs, out_specs=out_specs, check_vma=False)
```

```python
import functools

import jax
import jax.numpy as jnp
from jax import lax
from jax.experimental import pallas as pl
from jax.experimental.pallas import tpu as pltpu
from jax.sharding import Mesh
from jax.sharding import PartitionSpec as P


def dot(a, b):
    return jnp.dot(a, b, preferred_element_type=jnp.float32)


def adjoint_kernel(span, entry_ref, keep_ref, *refs):
    blocks, cot_ref, outs = refs[:4], refs[4], refs[5:9]
    x, square, iterate, left, right, grad_t, head, head_square, staged, arrived, sent = refs[9:]
    order, width = cot_ref.shape
    edge = order // width
    bf16, f32 = jnp.bfloat16, jnp.float32
    spans = [pl.ds(start, span) for start in range(0, order, span)]

    def at(index, size):
        return pl.ds(pl.multiple_of(index * size, size), size)

    def kept(block, entry):
        return block * keep_ref[entry].astype(f32).astype(bf16)

    room = staged.shape[1]
    arrivals = [
        pltpu.make_async_copy(block_ref, staged.at[source], arrived.at[source])
        for source, block_ref in enumerate(blocks)
    ]
    for copy in arrivals:
        copy.start()
    for source, copy in enumerate(arrivals):
        copy.wait()

        @pl.loop(0, room, unroll=4)
        def place(j, source=source):
            entry = entry_ref[source, j]
            x[at(entry // edge, width), at(entry % edge, width)] = kept(staged[source, j], entry)

    for c in spans:
        square[:, c] = dot(x[...], x[:, c]).astype(bf16)
    for c in spans:
        iterate[:, c] = (1.5 * x[:, c].astype(f32) - 0.5 * dot(x[...], square[:, c])).astype(bf16)

    one, two = width, 2 * width
    v, tail = 2 * two, 3 * two
    cot_t = cot_ref[...].astype(f32).T.astype(bf16)
    pulled_t = dot(cot_t, iterate[...]).astype(bf16)
    right[v : v + one, :] = pulled_t
    right[v + one : v + two, :] = cot_t
    left[:, :one] = iterate[:, :one]
    left[:, one:two] = dot(iterate[...], iterate[:, :one]).astype(bf16)
    left[:, tail : tail + one] = x[:, :one]
    left[:, tail + one :] = square[:, :one]
    head[...] = 1.5 * cot_t.astype(f32) - 0.5 * dot(pulled_t, iterate[...])
    right[tail + one :, :] = (-2.0 * head[...]).astype(bf16)
    rows = jnp.concatenate([right[v : v + two, :], right[tail + one :, :]])
    for c in spans:
        onto_x = dot(rows, x[:, c])
        right[two:v, c] = onto_x[:two].astype(bf16)
        right[tail : tail + one, c] = onto_x[two:].astype(bf16)
        onto_square = dot(rows, square[:, c])
        right[:two, c] = onto_square[:two].astype(bf16)
        head_square[:, c] = onto_square[two:]
    w = left[:, :two]
    left[:, two:v] = dot(x[...], w).astype(bf16)
    left[:, v:tail] = dot(square[...], w).astype(bf16)

    for c in spans:
        cot = -0.5 * dot(left[:, :two], right[v : v + two, c])
        rest = 0.25 * dot(left[...], right[:, c])
        top = (cot[:one] + head[:, c]).astype(bf16).astype(f32)
        grad_t[:one, c] = (1.5 * top + rest[:one] + 0.25 * head_square[:, c]).astype(bf16)
        grad_t[one:, c] = (1.5 * cot[one:].astype(bf16).astype(f32) + rest[one:]).astype(bf16)

    departures = []
    for target, out_ref in enumerate(outs):

        @pl.loop(0, room, unroll=4)
        def send(j, target=target):
            entry = entry_ref[len(blocks) + target, j]
            block = grad_t[at(entry % edge, width), at(entry // edge, width)]
            staged[target, j] = kept(block, entry)

        departures.append(pltpu.make_async_copy(staged.at[target], out_ref, sent.at[target]))
        departures[-1].start()
    for copy in departures:
        copy.wait()


def adjoint_pieces(entry, keep, blocks, cot, span=512):
    order, width = cot.shape
    room = blocks[0].shape[0]
    vmem = pl.BlockSpec(memory_space=pltpu.VMEM)
    anywhere = pl.BlockSpec(memory_space=pl.ANY)
    smem = pl.BlockSpec(memory_space=pltpu.SMEM)
    whole = pltpu.VMEM((order, order), jnp.bfloat16)
    strip = pltpu.VMEM((width, order), jnp.float32)
    return pl.pallas_call(
        functools.partial(adjoint_kernel, span),
        out_shape=[jax.ShapeDtypeStruct((room, width, width), jnp.bfloat16)] * 4,
        in_specs=[smem, smem] + [anywhere] * 4 + [vmem],
        out_specs=[anywhere] * 4,
        scratch_shapes=[whole] * 6
        + [strip] * 2
        + [pltpu.VMEM((4, room, width, width), jnp.bfloat16)]
        + [pltpu.SemaphoreType.DMA((4,))] * 2,
        compiler_params=pltpu.CompilerParams(vmem_limit_bytes=40 << 20),
        cost_estimate=pl.CostEstimate(flops=11_000_000_000, bytes_accessed=5 << 20, transcendentals=0),
    )(entry, keep, *blocks, cot)


def arrange(index, sources, counts):
    split = len(sources) == 1
    fixed = counts if split else [source.shape[0] for source in sources]
    given, total = sum(source.shape[0] for source in sources), sum(counts)

    def kernel(index_ref, *refs):
        ins, outs = refs[: len(sources)], refs[len(sources) : len(sources) + len(counts)]
        came, leaves, arrived, sent = refs[len(sources) + len(counts) :]

        def bulk(ref, place, staged, start, done, inward):
            part = staged.at[pl.ds(start, ref.shape[0])]
            pair = (ref, part) if inward else (part, ref)
            return pltpu.make_async_copy(*pair, done.at[place])

        def starts(refs):
            return [sum(ref.shape[0] for ref in refs[:place]) for place in range(len(refs))]

        arrivals = [bulk(ref, i, came, s, arrived, True) for i, (ref, s) in enumerate(zip(ins, starts(ins)))]
        departures = [bulk(ref, i, leaves, s, sent, False) for i, (ref, s) in enumerate(zip(outs, starts(outs)))]
        for copy in arrivals:
            copy.start()
        start = 0
        for place, count in enumerate(fixed):
            if place < len(arrivals):
                arrivals[place].wait()

            @pl.loop(0, count, unroll=4)
            def _(j, start=start):
                spot = index_ref[start + j]
                if split:
                    leaves[start + j] = came[spot]
                else:
                    leaves[spot] = came[start + j]

            start += count
            if split:
                departures[place].start()
        if not split:
            departures[0].start()
        for copy in departures:
            copy.wait()

    anywhere = pl.BlockSpec(memory_space=pl.ANY)
    shape, dtype = sources[0].shape[1:], sources[0].dtype
    return pl.pallas_call(
        kernel,
        out_shape=[jax.ShapeDtypeStruct((count, *shape), dtype) for count in counts],
        in_specs=[pl.BlockSpec(memory_space=pltpu.SMEM)] + [anywhere] * len(sources),
        out_specs=[anywhere] * len(counts),
        scratch_shapes=[pltpu.VMEM((given, *shape), dtype), pltpu.VMEM((total, *shape), dtype)]
        + [pltpu.SemaphoreType.DMA((len(sources),)), pltpu.SemaphoreType.DMA((len(counts),))],
        compiler_params=pltpu.CompilerParams(vmem_limit_bytes=16 << 20),
        cost_estimate=pl.CostEstimate(flops=0, bytes_accessed=4 << 20, transcendentals=0),
    )(index, *sources)


AXES = ("x", "z", "core", "y")
SIZES = dict(x=4, z=8, core=2, y=4)


def shift(blocks, axis, step):
    count = SIZES[axis]
    return lax.ppermute(blocks, axis, [(i, (i + step) % count) for i in range(count)])


def picked_sum(hits, values):
    return jnp.sum(jnp.where(hits, values, 0), axis=-1)


def tables(block_ids, slot_count):
    nx, nz, nk, ny = (SIZES[a] for a in AXES)
    mx, mz, mk, my = (lax.axis_index(a) for a in AXES)
    entries = block_ids.shape[1]
    room = entries // ny
    by_place = block_ids.reshape(nx, nz, nk, ny * entries)
    level = lax.dynamic_index_in_dim(by_place, mz, 1, keepdims=False)
    owner, slot = level // slot_count, level % slot_count
    oy, ok, oz, ox = owner % ny, owner // ny % nk, owner // (ny * nk) % nz, owner // (ny * nk * nz)
    asked = (ox == mx) & (ok == mk) & (oy == my)
    far = jnp.where(asked, (oz - mz) % nz, nz)
    slots = picked_sum(far[:, :, None, :] == jnp.arange(nz)[:, None], slot[:, :, None, :])
    slots = jnp.roll(jnp.roll(slots, -mx, axis=0), -mk, axis=1)

    def mine(a):
        a = lax.dynamic_index_in_dim(a, mx, 0, keepdims=False)
        return lax.dynamic_index_in_dim(a, mk, 0, keepdims=False).reshape(ny, entries)

    oy, ok, oz, ox = mine(oy), mine(ok), mine(oz), mine(ox)
    stand = (((ok - mk) % nk) * nx + (mx - ox) % nx) * nz + (oz - mz) % nz
    stand = jnp.roll(stand, -my, axis=0)
    here = jnp.roll(oy == my, -my, axis=0)
    rank = jnp.cumsum(here.astype(jnp.int32), axis=1) - 1
    rank = jnp.where(here, rank, room)
    place = picked_sum(rank[:, None, :] == jnp.arange(room)[:, None], stand[:, None, :])
    mine_y = lax.dynamic_index_in_dim(oy, my, 0, keepdims=False)
    there = (mine_y[None, :] - my) % ny == jnp.arange(ny)[:, None]
    rank = jnp.cumsum(there.astype(jnp.int32), axis=1) - 1
    rank = jnp.where(there, rank, room)
    entry = picked_sum(rank[:, None, :] == jnp.arange(room)[:, None], jnp.arange(entries))
    return slots, place, entry


def shards(h_blocks, block_ids, pattern, result_grad):
    nx, nz, nk, ny = (SIZES[a] for a in AXES)
    slot_count, width, _ = h_blocks.shape
    entries = block_ids.shape[1]
    room = entries // ny
    slots, place, entry = tables(block_ids, slot_count)

    mx, mz, mk = (lax.axis_index(a) for a in AXES[:3])

    def over_row(blocks):
        return lax.all_to_all(blocks, AXES[:3], split_axis=0, concat_axis=0, tiled=True)

    level_x, level_z, level_k = jnp.meshgrid(jnp.arange(nx), jnp.arange(nz), jnp.arange(nk), indexing="ij")
    stand = ((((level_k - mk) % nk) * nx + (mx - level_x) % nx) * nz + (level_z - mz) % nz).reshape(-1)
    mine = block_ids // slot_count == (lax.axis_index(AXES[:3]) * ny + lax.axis_index("y"))
    asked = jnp.sum(jnp.where(mine, block_ids % slot_count, 0).reshape(entries, -1), axis=1)
    row_of_stand = picked_sum(stand[None, :] == jnp.arange(entries)[:, None], jnp.arange(entries))
    place = picked_sum(
        place.reshape(-1)[:, None] == jnp.arange(entries), row_of_stand
    ).reshape(place.shape)
    (asked_blocks,) = arrange(asked, [h_blocks], [entries])
    held = over_row(asked_blocks)

    order = jnp.concatenate([place[1], place[3], place[2], place[0]])
    ahead, behind, across, own = arrange(order, [held], [room] * ny)
    near, back, far = shift(ahead, "y", 1), shift(behind, "y", -1), shift(across, "y", 2)
    turned = jnp.stack([entry[i] for i in (0, 3, 1, 2, 1, 3, 2, 0)])
    ahead, behind, across, own = adjoint_pieces(
        turned, pattern.reshape(-1), [own, near, back, far], result_grad
    )
    near, back, far = shift(ahead, "y", 1), shift(behind, "y", -1), shift(across, "y", 2)
    order = jnp.concatenate([place[3], place[1], place[2], place[0]])
    (held,) = arrange(order, [near, back, far, own], [entries])

    held = over_row(held)
    weights = (asked[None, :] == jnp.arange(slot_count)[:, None]).astype(jnp.bfloat16)
    return jnp.einsum("sr,rab->sba", weights, held, preferred_element_type=jnp.float32)


def solution(mesh):
    torus = Mesh(mesh.devices.reshape([SIZES[a] for a in AXES]), AXES)
    in_specs = (P(AXES, None, None), P(), P(AXES, None, None), P(AXES, None))
    return jax.shard_map(
        shards, mesh=torus, in_specs=in_specs, out_specs=P(AXES, None, None), check_vma=False
    )
```

```python
import functools

import jax
import jax.numpy as jnp
from jax import lax
from jax.experimental import pallas as pl
from jax.experimental.pallas import tpu as pltpu
from jax.sharding import Mesh
from jax.sharding import PartitionSpec as P


def dot(a, b):
    return jnp.dot(a, b, preferred_element_type=jnp.float32)


def starts_of(refs):
    sizes = [ref.shape[0] for ref in refs]
    return [sum(sizes[:place]) for place in range(len(sizes))]


def bulk(refs, staged, done, inward):
    copies = []
    for place, (ref, start) in enumerate(zip(refs, starts_of(refs))):
        part = staged.at[pl.ds(start, ref.shape[0])]
        pair = (ref, part) if inward else (part, ref)
        copies.append(pltpu.make_async_copy(*pair, done.at[place]))
    return copies


def adjoint_kernel(span, arrays, entry_ref, keep_ref, *refs):
    blocks, cot_ref, outs = refs[:arrays], refs[arrays], refs[arrays + 1 : 2 * arrays + 1]
    x, square, iterate, left, right, grad_t, head, head_square, staged, arrived, sent = refs[
        2 * arrays + 1 :
    ]
    order, width = cot_ref.shape
    edge = order // width
    bf16, f32 = jnp.bfloat16, jnp.float32
    spans = [pl.ds(start, span) for start in range(0, order, span)]

    def at(index, size):
        return pl.ds(pl.multiple_of(index * size, size), size)

    def kept(block, entry):
        return block * keep_ref[entry].astype(f32).astype(bf16)

    arrivals = bulk(blocks, staged, arrived, True)
    for copy in arrivals:
        copy.start()
    for copy, ref, start in zip(arrivals, blocks, starts_of(blocks)):
        copy.wait()

        @pl.loop(start, start + ref.shape[0], unroll=4)
        def place(j):
            entry = entry_ref[0, j]
            x[at(entry // edge, width), at(entry % edge, width)] = kept(staged[j], entry)

    for c in spans:
        square[:, c] = dot(x[...], x[:, c]).astype(bf16)
    for c in spans:
        iterate[:, c] = (1.5 * x[:, c].astype(f32) - 0.5 * dot(x[...], square[:, c])).astype(bf16)

    one, two = width, 2 * width
    v, tail = 2 * two, 3 * two
    cot_t = cot_ref[...].astype(f32).T.astype(bf16)
    pulled_t = dot(cot_t, iterate[...]).astype(bf16)
    right[v : v + one, :] = pulled_t
    right[v + one : v + two, :] = cot_t
    left[:, :one] = iterate[:, :one]
    left[:, one:two] = dot(iterate[...], iterate[:, :one]).astype(bf16)
    left[:, tail : tail + one] = x[:, :one]
    left[:, tail + one :] = square[:, :one]
    head[...] = 1.5 * cot_t.astype(f32) - 0.5 * dot(pulled_t, iterate[...])
    right[tail + one :, :] = (-2.0 * head[...]).astype(bf16)
    rows = jnp.concatenate([right[v : v + two, :], right[tail + one :, :]])
    for c in spans:
        onto_x = dot(rows, x[:, c])
        right[two:v, c] = onto_x[:two].astype(bf16)
        right[tail : tail + one, c] = onto_x[two:].astype(bf16)
        onto_square = dot(rows, square[:, c])
        right[:two, c] = onto_square[:two].astype(bf16)
        head_square[:, c] = onto_square[two:]
    w = left[:, :two]
    left[:, two:v] = dot(x[...], w).astype(bf16)
    left[:, v:tail] = dot(square[...], w).astype(bf16)

    for c in spans:
        cot = -0.5 * dot(left[:, :two], right[v : v + two, c])
        rest = 0.25 * dot(left[...], right[:, c])
        top = (cot[:one] + head[:, c]).astype(bf16).astype(f32)
        grad_t[:one, c] = (1.5 * top + rest[:one] + 0.25 * head_square[:, c]).astype(bf16)
        grad_t[one:, c] = (1.5 * cot[one:].astype(bf16).astype(f32) + rest[one:]).astype(bf16)

    departures = bulk(outs, staged, sent, False)
    for copy, ref, start in zip(departures, outs, starts_of(outs)):

        @pl.loop(start, start + ref.shape[0], unroll=4)
        def send(j):
            entry = entry_ref[1, j]
            block = grad_t[at(entry % edge, width), at(entry // edge, width)]
            staged[j] = kept(block, entry)

        copy.start()
    for copy in departures:
        copy.wait()


def adjoint_pieces(entry, keep, blocks, cot, counts, span=512):
    order, width = cot.shape
    arrays = len(blocks)
    anywhere = pl.BlockSpec(memory_space=pl.ANY)
    smem = pl.BlockSpec(memory_space=pltpu.SMEM)
    whole = pltpu.VMEM((order, order), jnp.bfloat16)
    strip = pltpu.VMEM((width, order), jnp.float32)
    return pl.pallas_call(
        functools.partial(adjoint_kernel, span, arrays),
        out_shape=[jax.ShapeDtypeStruct((count, width, width), jnp.bfloat16) for count in counts],
        in_specs=[smem, smem] + [anywhere] * arrays + [pl.BlockSpec(memory_space=pltpu.VMEM)],
        out_specs=[anywhere] * arrays,
        scratch_shapes=[whole] * 6
        + [strip] * 2
        + [pltpu.VMEM((sum(counts), width, width), jnp.bfloat16)]
        + [pltpu.SemaphoreType.DMA((arrays,))] * 2,
        compiler_params=pltpu.CompilerParams(vmem_limit_bytes=40 << 20),
        cost_estimate=pl.CostEstimate(flops=11_000_000_000, bytes_accessed=5 << 20, transcendentals=0),
    )(entry, keep, *blocks, cot)


def arrange(index, sources, counts, into_source_order=False, outside=pl.ANY):
    given, total = sum(source.shape[0] for source in sources), sum(counts)

    def kernel(index_ref, *refs):
        ins, outs = refs[: len(sources)], refs[len(sources) : len(sources) + len(counts)]
        came, leaves, arrived, sent = refs[len(sources) + len(counts) :]
        arrivals = bulk(ins, came, arrived, True)
        departures = bulk(outs, leaves, sent, False)
        for copy in arrivals:
            copy.start()
        if into_source_order:
            for copy, ref, start in zip(arrivals, ins, starts_of(ins)):
                copy.wait()

                @pl.loop(start, start + ref.shape[0], unroll=4)
                def _(j):
                    leaves[index_ref[j]] = came[j]

            departures[0].start()
        else:
            for copy in arrivals:
                copy.wait()
            for copy, ref, start in zip(departures, outs, starts_of(outs)):

                @pl.loop(start, start + ref.shape[0], unroll=4 if ref.shape[0] % 4 == 0 else 2)
                def _(j):
                    leaves[j] = came[index_ref[j]]

                copy.start()
        for copy in departures:
            copy.wait()

    shape, dtype = sources[0].shape[1:], sources[0].dtype
    return pl.pallas_call(
        kernel,
        out_shape=[jax.ShapeDtypeStruct((count, *shape), dtype) for count in counts],
        in_specs=[pl.BlockSpec(memory_space=pltpu.SMEM)]
        + [pl.BlockSpec(memory_space=outside)] * len(sources),
        out_specs=[pl.BlockSpec(memory_space=outside)] * len(counts),
        scratch_shapes=[pltpu.VMEM((given, *shape), dtype), pltpu.VMEM((total, *shape), dtype)]
        + [pltpu.SemaphoreType.DMA((len(sources),)), pltpu.SemaphoreType.DMA((len(counts),))],
        compiler_params=pltpu.CompilerParams(vmem_limit_bytes=16 << 20),
        cost_estimate=pl.CostEstimate(flops=0, bytes_accessed=4 << 20, transcendentals=0),
    )(index, *sources)


AXES = ("x", "z", "core", "y")
SIZES = dict(x=4, z=8, core=2, y=4)
FIRST_LATE, LATE = 3, 3


def shift(blocks, axis, step):
    count = SIZES[axis]
    return lax.ppermute(blocks, axis, [(i, (i + step) % count) for i in range(count)])


def picked_sum(hits, values):
    return jnp.sum(jnp.where(hits, values, 0), axis=-1)


def tables(block_ids, slot_count):
    nx, nz, nk, ny = (SIZES[a] for a in AXES)
    mx, mz, mk, my = (lax.axis_index(a) for a in AXES)
    entries = block_ids.shape[1]
    room = entries // ny
    owners = block_ids // slot_count
    mine = owners == ((mx * nz + mz) * nk + mk) * ny + my
    asked = jnp.sum(jnp.where(mine, block_ids % slot_count, 0).reshape(nx * nz * nk, -1), axis=1)
    by_place = block_ids.reshape(nx, nz, nk, ny * entries)
    level = lax.dynamic_index_in_dim(by_place, mz, 1, keepdims=False)
    owner, slot = level // slot_count, level % slot_count
    row, oy = owner // ny, owner % ny
    ok, oz, ox = row % nk, row // nk % nz, row // (nk * nz)
    far = jnp.where((ox == mx) & (ok == mk) & (oy == my), (oz - mz) % nz, nz)
    slots = picked_sum(far[:, :, None, :] == jnp.arange(nz)[:, None], slot[:, :, None, :])
    slots = jnp.roll(jnp.roll(slots, -mx, axis=0), -mk, axis=1)

    def of_my_row(a):
        a = lax.dynamic_index_in_dim(a, mx, 0, keepdims=False)
        return lax.dynamic_index_in_dim(a, mk, 0, keepdims=False).reshape(ny, entries)

    row, oy, ok, oz, ox = (of_my_row(a) for a in (row, oy, ok, oz, ox))
    dk, dz, dx = (ok - mk) % nk, (oz - mz) % nz, (mx - ox) % nx
    late = (dz >= FIRST_LATE) & (dz < FIRST_LATE + LATE)
    early = nz - LATE
    group = jnp.where(late, LATE, early)
    within = jnp.where(dz < FIRST_LATE, dz, jnp.where(late, dz - FIRST_LATE, dz - LATE))
    stand = jnp.where(late, (nk + 1) * nx * early, 0) + within
    lane = jnp.where(dx == 0, 3, jnp.where(dx == 1, 0, jnp.where(dx == 3, 1, 2)))
    stand = stand + jnp.where(dk == 0, lane * nk, nk * nx + lane) * group
    here = oy == my
    rank = jnp.where(here, jnp.cumsum(here.astype(jnp.int32), axis=1) - 1, room)
    hits = rank[:, None, :] == jnp.arange(room)[:, None]
    ring = jnp.roll(picked_sum(hits, stand[:, None, :]), -my, axis=0)
    rows = jnp.roll(picked_sum(hits, row[:, None, :]), -my, axis=0)
    mine_y = lax.dynamic_index_in_dim(oy, my, 0, keepdims=False)
    there = (mine_y[None, :] - my) % ny == jnp.arange(ny)[:, None]
    rank = jnp.where(there, jnp.cumsum(there.astype(jnp.int32), axis=1) - 1, room)
    entry = picked_sum(rank[:, None, :] == jnp.arange(room)[:, None], jnp.arange(entries))
    return slots, asked, ring, rows, entry


def shards(h_blocks, block_ids, pattern, result_grad):
    nx, nz, nk, ny = (SIZES[a] for a in AXES)
    slot_count, width, _ = h_blocks.shape
    entries = block_ids.shape[1]
    room = entries // ny
    slots, asked, ring, rows, entry = tables(block_ids, slot_count)

    half = slot_count // 2
    up, down = [h_blocks], [h_blocks]
    for _ in range(nz // 2 - 1):
        up.append(shift(up[-1], "z", 1))
        down.append(shift(down[-1], "z", -1))
    up.append(shift(up[-1][:half], "z", 1))
    down.append(shift(down[-1][half:], "z", -1))
    early = [*down[:FIRST_LATE], up[2], up[1]]
    late = [down[3], up[4], down[4], up[3]]
    end = FIRST_LATE + LATE
    early_slots = jnp.concatenate([slots[:, :, :FIRST_LATE], slots[:, :, end:]], axis=2)

    def over_x_and_core(sources, wanted):
        size = wanted.shape[2]
        wanted = wanted + slot_count * jnp.arange(size)
        order = jnp.concatenate([wanted[i].reshape(-1) for i in (1, 3, 2, 0)])
        ahead, behind, across, own = arrange(order, sources, [nk * size] * nx)
        came = [shift(ahead, "x", 1), shift(behind, "x", -1), shift(across, "x", 2), own]
        other = jnp.concatenate([part[size:] for part in came])
        return [*came, shift(other, "core", 1)]

    held = over_x_and_core(early, early_slots)
    held = held + over_x_and_core(late, slots[:, :, FIRST_LATE:end])

    routes = [(step, room // 1) for step in (1, -1, 2) for _ in range(1)]
    counts = [count for _, count in routes] + [room]

    def over_col(parts):
        return [shift(part, "y", step) for part, (step, _) in zip(parts, routes)] + [parts[-1]]

    order = jnp.concatenate([ring[i] for i in (1, 3, 2, 0)])
    blocks = over_col(arrange(order, held, counts))
    came = jnp.concatenate([entry[i] for i in (3, 1, 2, 0)])
    leaves = jnp.concatenate([entry[i] for i in (1, 3, 2, 0)])
    pieces = adjoint_pieces(
        jnp.stack([came, leaves]), pattern.reshape(-1), blocks, result_grad, counts
    )
    order = jnp.concatenate([rows[i] for i in (3, 1, 2, 0)])
    (held,) = arrange(order, over_col(pieces), [entries], into_source_order=True)

    held = lax.all_to_all(held, AXES[:3], split_axis=0, concat_axis=0, tiled=True)
    weights = (asked[None, :] == jnp.arange(slot_count)[:, None]).astype(jnp.bfloat16)
    return jnp.einsum("sr,rab->sba", weights, held, preferred_element_type=jnp.float32)


def solution(mesh):
    torus = Mesh(mesh.devices.reshape([SIZES[a] for a in AXES]), AXES)
    in_specs = (P(AXES, None, None), P(), P(AXES, None, None), P(AXES, None))
    return jax.shard_map(
        shards, mesh=torus, in_specs=in_specs, out_specs=P(AXES, None, None), check_vma=False
    )
```

```python
import functools

import jax
import jax.numpy as jnp
from jax import lax
from jax.experimental import pallas as pl
from jax.experimental.pallas import tpu as pltpu
from jax.sharding import Mesh
from jax.sharding import PartitionSpec as P


def dot(a, b):
    return jnp.dot(a, b, preferred_element_type=jnp.float32)


def starts_of(refs):
    sizes = [ref.shape[0] for ref in refs]
    return [sum(sizes[:place]) for place in range(len(sizes))]


def bulk(refs, staged, done, inward):
    copies = []
    for place, (ref, start) in enumerate(zip(refs, starts_of(refs))):
        part = staged.at[pl.ds(start, ref.shape[0])]
        pair = (ref, part) if inward else (part, ref)
        copies.append(pltpu.make_async_copy(*pair, done.at[place]))
    return copies


def adjoint_kernel(span, arrays, entry_ref, keep_ref, *refs):
    blocks, cot_ref, outs = refs[:arrays], refs[arrays], refs[arrays + 1 : 2 * arrays + 1]
    x, square, iterate, left, right, grad_t, head, head_square, staged, arrived, sent = refs[
        2 * arrays + 1 :
    ]
    order, width = cot_ref.shape
    edge = order // width
    bf16, f32 = jnp.bfloat16, jnp.float32
    spans = [pl.ds(start, span) for start in range(0, order, span)]

    def at(index, size):
        return pl.ds(pl.multiple_of(index * size, size), size)

    def kept(block, entry):
        return block * keep_ref[entry].astype(f32).astype(bf16)

    arrivals = bulk(blocks, staged, arrived, True)
    for copy in arrivals:
        copy.start()
    for copy, ref, start in zip(arrivals, blocks, starts_of(blocks)):
        copy.wait()

        @pl.loop(start, start + ref.shape[0], unroll=16)
        def place(j):
            entry = entry_ref[0, j]
            x[at(entry // edge, width), at(entry % edge, width)] = kept(staged[j], entry)

    for c in spans:
        square[:, c] = dot(x[...], x[:, c]).astype(bf16)
    for c in spans:
        iterate[:, c] = (1.5 * x[:, c].astype(f32) - 0.5 * dot(x[...], square[:, c])).astype(bf16)

    one, two = width, 2 * width
    v, tail = 2 * two, 3 * two
    cot_t = cot_ref[...].astype(f32).T.astype(bf16)
    pulled_t = dot(cot_t, iterate[...]).astype(bf16)
    right[v : v + one, :] = pulled_t
    right[v + one : v + two, :] = cot_t
    left[:, :one] = iterate[:, :one]
    left[:, one:two] = dot(iterate[...], iterate[:, :one]).astype(bf16)
    left[:, tail : tail + one] = x[:, :one]
    left[:, tail + one :] = square[:, :one]
    head[...] = 1.5 * cot_t.astype(f32) - 0.5 * dot(pulled_t, iterate[...])
    right[tail + one :, :] = (-2.0 * head[...]).astype(bf16)
    rows = jnp.concatenate([right[v : v + two, :], right[tail + one :, :]])
    for c in spans:
        onto_x = dot(rows, x[:, c])
        right[two:v, c] = onto_x[:two].astype(bf16)
        right[tail : tail + one, c] = onto_x[two:].astype(bf16)
        onto_square = dot(rows, square[:, c])
        right[:two, c] = onto_square[:two].astype(bf16)
        head_square[:, c] = onto_square[two:]
    w = left[:, :two]
    left[:, two:v] = dot(x[...], w).astype(bf16)
    left[:, v:tail] = dot(square[...], w).astype(bf16)

    for c in spans:
        cot = -0.5 * dot(left[:, :two], right[v : v + two, c])
        rest = 0.25 * dot(left[...], right[:, c])
        top = (cot[:one] + head[:, c]).astype(bf16).astype(f32)
        grad_t[:one, c] = (1.5 * top + rest[:one] + 0.25 * head_square[:, c]).astype(bf16)
        grad_t[one:, c] = (1.5 * cot[one:].astype(bf16).astype(f32) + rest[one:]).astype(bf16)

    departures = bulk(outs, staged, sent, False)
    for copy, ref, start in zip(departures, outs, starts_of(outs)):

        @pl.loop(start, start + ref.shape[0], unroll=16)
        def send(j):
            entry = entry_ref[1, j]
            block = grad_t[at(entry % edge, width), at(entry // edge, width)]
            staged[j] = kept(block, entry)

        copy.start()
    for copy in departures:
        copy.wait()


def adjoint_pieces(entry, keep, blocks, cot, counts, span=512):
    order, width = cot.shape
    arrays = len(blocks)
    anywhere = pl.BlockSpec(memory_space=pl.ANY)
    smem = pl.BlockSpec(memory_space=pltpu.SMEM)
    whole = pltpu.VMEM((order, order), jnp.bfloat16)
    strip = pltpu.VMEM((width, order), jnp.float32)
    return pl.pallas_call(
        functools.partial(adjoint_kernel, span, arrays),
        out_shape=[jax.ShapeDtypeStruct((count, width, width), jnp.bfloat16) for count in counts],
        in_specs=[smem, smem] + [anywhere] * arrays + [pl.BlockSpec(memory_space=pltpu.VMEM)],
        out_specs=[anywhere] * arrays,
        scratch_shapes=[whole] * 6
        + [strip] * 2
        + [pltpu.VMEM((sum(counts), width, width), jnp.bfloat16)]
        + [pltpu.SemaphoreType.DMA((arrays,))] * 2,
        compiler_params=pltpu.CompilerParams(vmem_limit_bytes=40 << 20),
        cost_estimate=pl.CostEstimate(flops=11_000_000_000, bytes_accessed=5 << 20, transcendentals=0),
    )(entry, keep, *blocks, cot)


def arrange(index, sources, counts, into_source_order=False, outside=pl.ANY):
    given, total = sum(source.shape[0] for source in sources), sum(counts)

    def kernel(index_ref, *refs):
        ins, outs = refs[: len(sources)], refs[len(sources) : len(sources) + len(counts)]
        came, leaves, arrived, sent = refs[len(sources) + len(counts) :]
        arrivals = bulk(ins, came, arrived, True)
        departures = bulk(outs, leaves, sent, False)
        for copy in arrivals:
            copy.start()
        if into_source_order:
            for copy, ref, start in zip(arrivals, ins, starts_of(ins)):
                copy.wait()

                @pl.loop(start, start + ref.shape[0], unroll=16)
                def _(j):
                    leaves[index_ref[j]] = came[j]

            departures[0].start()
        else:
            for copy in arrivals:
                copy.wait()
            for copy, ref, start in zip(departures, outs, starts_of(outs)):

                @pl.loop(start, start + ref.shape[0], unroll=4 if ref.shape[0] % 4 == 0 else 2)
                def _(j):
                    leaves[j] = came[index_ref[j]]

                copy.start()
        for copy in departures:
            copy.wait()

    shape, dtype = sources[0].shape[1:], sources[0].dtype
    return pl.pallas_call(
        kernel,
        out_shape=[jax.ShapeDtypeStruct((count, *shape), dtype) for count in counts],
        in_specs=[pl.BlockSpec(memory_space=pltpu.SMEM)]
        + [pl.BlockSpec(memory_space=outside)] * len(sources),
        out_specs=[pl.BlockSpec(memory_space=outside)] * len(counts),
        scratch_shapes=[pltpu.VMEM((given, *shape), dtype), pltpu.VMEM((total, *shape), dtype)]
        + [pltpu.SemaphoreType.DMA((len(sources),)), pltpu.SemaphoreType.DMA((len(counts),))],
        compiler_params=pltpu.CompilerParams(vmem_limit_bytes=16 << 20),
        cost_estimate=pl.CostEstimate(flops=0, bytes_accessed=4 << 20, transcendentals=0),
    )(index, *sources)


AXES = ("x", "z", "core", "y")
SIZES = dict(x=4, z=8, core=2, y=4)
FIRST_LATE, LATE = 3, 3


def shift(blocks, axis, step):
    count = SIZES[axis]
    return lax.ppermute(blocks, axis, [(i, (i + step) % count) for i in range(count)])


def picked_sum(hits, values):
    return jnp.sum(jnp.where(hits, values, 0), axis=-1)


def tables(block_ids, slot_count):
    nx, nz, nk, ny = (SIZES[a] for a in AXES)
    mx, mz, mk, my = (lax.axis_index(a) for a in AXES)
    entries = block_ids.shape[1]
    room = entries // ny
    owners = block_ids // slot_count
    mine = owners == ((mx * nz + mz) * nk + mk) * ny + my
    asked = jnp.sum(jnp.where(mine, block_ids % slot_count, 0).reshape(nx * nz * nk, -1), axis=1)
    by_place = block_ids.reshape(nx, nz, nk, ny * entries)
    level = lax.dynamic_index_in_dim(by_place, mz, 1, keepdims=False)
    owner, slot = level // slot_count, level % slot_count
    row, oy = owner // ny, owner % ny
    ok, oz, ox = row % nk, row // nk % nz, row // (nk * nz)
    far = jnp.where((ox == mx) & (ok == mk) & (oy == my), (oz - mz) % nz, nz)
    slots = picked_sum(far[:, :, None, :] == jnp.arange(nz)[:, None], slot[:, :, None, :])
    slots = jnp.roll(jnp.roll(slots, -mx, axis=0), -mk, axis=1)

    def of_my_row(a):
        a = lax.dynamic_index_in_dim(a, mx, 0, keepdims=False)
        return lax.dynamic_index_in_dim(a, mk, 0, keepdims=False).reshape(ny, entries)

    row, oy, ok, oz, ox = (of_my_row(a) for a in (row, oy, ok, oz, ox))
    dk, dz, dx = (ok - mk) % nk, (oz - mz) % nz, (mx - ox) % nx
    late = (dz >= FIRST_LATE) & (dz < FIRST_LATE + LATE)
    early = nz - LATE
    group = jnp.where(late, LATE, early)
    within = jnp.where(dz < FIRST_LATE, dz, jnp.where(late, dz - FIRST_LATE, dz - LATE))
    stand = jnp.where(late, (nk + 1) * nx * early, 0) + within
    lane = jnp.where(dx == 0, 3, jnp.where(dx == 1, 0, jnp.where(dx == 3, 1, 2)))
    stand = stand + jnp.where(dk == 0, lane * nk, nk * nx + lane) * group
    here = oy == my
    rank = jnp.where(here, jnp.cumsum(here.astype(jnp.int32), axis=1) - 1, room)
    hits = rank[:, None, :] == jnp.arange(room)[:, None]
    ring = jnp.roll(picked_sum(hits, stand[:, None, :]), -my, axis=0)
    rows = jnp.roll(picked_sum(hits, row[:, None, :]), -my, axis=0)
    mine_y = lax.dynamic_index_in_dim(oy, my, 0, keepdims=False)
    there = (mine_y[None, :] - my) % ny == jnp.arange(ny)[:, None]
    rank = jnp.where(there, jnp.cumsum(there.astype(jnp.int32), axis=1) - 1, room)
    entry = picked_sum(rank[:, None, :] == jnp.arange(room)[:, None], jnp.arange(entries))
    return slots, asked, ring, rows, entry


def shards(h_blocks, block_ids, pattern, result_grad):
    nx, nz, nk, ny = (SIZES[a] for a in AXES)
    slot_count, width, _ = h_blocks.shape
    entries = block_ids.shape[1]
    room = entries // ny
    slots, asked, ring, rows, entry = tables(block_ids, slot_count)

    half = slot_count // 2
    up, down = [h_blocks], [h_blocks]
    for _ in range(nz // 2 - 1):
        up.append(shift(up[-1], "z", 1))
        down.append(shift(down[-1], "z", -1))
    up.append(shift(up[-1][:half], "z", 1))
    down.append(shift(down[-1][half:], "z", -1))
    early = [*down[:FIRST_LATE], up[2], up[1]]
    late = [down[3], up[4], down[4], up[3]]
    end = FIRST_LATE + LATE
    early_slots = jnp.concatenate([slots[:, :, :FIRST_LATE], slots[:, :, end:]], axis=2)

    def over_x_and_core(sources, wanted):
        size = wanted.shape[2]
        wanted = wanted + slot_count * jnp.arange(size)
        order = jnp.concatenate([wanted[i].reshape(-1) for i in (1, 3, 2, 0)])
        ahead, behind, across, own = arrange(order, sources, [nk * size] * nx)
        came = [shift(ahead, "x", 1), shift(behind, "x", -1), shift(across, "x", 2), own]
        other = jnp.concatenate([part[size:] for part in came])
        return [*came, shift(other, "core", 1)]

    held = over_x_and_core(early, early_slots)
    held = held + over_x_and_core(late, slots[:, :, FIRST_LATE:end])

    routes = [(step, room // 1) for step in (1, -1, 2) for _ in range(1)]
    counts = [count for _, count in routes] + [room]

    def over_col(parts):
        return [shift(part, "y", step) for part, (step, _) in zip(parts, routes)] + [parts[-1]]

    order = jnp.concatenate([ring[i] for i in (1, 3, 2, 0)])
    blocks = over_col(arrange(order, held, counts))
    came = jnp.concatenate([entry[i] for i in (3, 1, 2, 0)])
    leaves = jnp.concatenate([entry[i] for i in (1, 3, 2, 0)])
    pieces = adjoint_pieces(
        jnp.stack([came, leaves]), pattern.reshape(-1), blocks, result_grad, counts
    )
    order = jnp.concatenate([rows[i] for i in (3, 1, 2, 0)])
    (held,) = arrange(order, over_col(pieces), [entries], into_source_order=True)

    held = lax.all_to_all(held, AXES[:3], split_axis=0, concat_axis=0, tiled=True)
    weights = (asked[None, :] == jnp.arange(slot_count)[:, None]).astype(jnp.bfloat16)
    return jnp.einsum("sr,rab->sba", weights, held, preferred_element_type=jnp.float32)


def solution(mesh):
    torus = Mesh(mesh.devices.reshape([SIZES[a] for a in AXES]), AXES)
    in_specs = (P(AXES, None, None), P(), P(AXES, None, None), P(AXES, None))
    return jax.shard_map(
        shards, mesh=torus, in_specs=in_specs, out_specs=P(AXES, None, None), check_vma=False
    )
```

```python
import functools

import jax
import jax.numpy as jnp
from jax import lax
from jax.experimental import pallas as pl
from jax.experimental.pallas import tpu as pltpu
from jax.sharding import Mesh
from jax.sharding import PartitionSpec as P


def dot(a, b):
    return jnp.dot(a, b, preferred_element_type=jnp.float32)


def starts_of(refs):
    sizes = [ref.shape[0] for ref in refs]
    return [sum(sizes[:place]) for place in range(len(sizes))]


def bulk(refs, staged, done, inward):
    copies = []
    for place, (ref, start) in enumerate(zip(refs, starts_of(refs))):
        part = staged.at[pl.ds(start, ref.shape[0])]
        pair = (ref, part) if inward else (part, ref)
        copies.append(pltpu.make_async_copy(*pair, done.at[place]))
    return copies


def adjoint_kernel(span, arrays, entry_ref, keep_ref, *refs):
    blocks, cot_ref, outs = refs[:arrays], refs[arrays], refs[arrays + 1 : 2 * arrays + 1]
    x, square, iterate, left, right, grad_t, head, head_square, staged, arrived, sent = refs[
        2 * arrays + 1 :
    ]
    order, width = cot_ref.shape
    edge = order // width
    bf16, f32 = jnp.bfloat16, jnp.float32
    spans = [pl.ds(start, span) for start in range(0, order, span)]

    def at(index, size):
        return pl.ds(pl.multiple_of(index * size, size), size)

    def kept(block, entry):
        return block * keep_ref[entry].astype(f32).astype(bf16)

    arrivals = bulk(blocks, staged, arrived, True)
    for copy in arrivals:
        copy.start()
    for copy, ref, start in zip(arrivals, blocks, starts_of(blocks)):
        copy.wait()

        @pl.loop(start, start + ref.shape[0], unroll=16)
        def place(j):
            entry = entry_ref[0, j]
            x[at(entry // edge, width), at(entry % edge, width)] = kept(staged[j], entry)

    for c in spans:
        square[:, c] = dot(x[...], x[:, c]).astype(bf16)
    for c in spans:
        iterate[:, c] = (1.5 * x[:, c].astype(f32) - 0.5 * dot(x[...], square[:, c])).astype(bf16)

    one, two = width, 2 * width
    v, tail = 2 * two, 3 * two
    cot_t = cot_ref[...].astype(f32).T.astype(bf16)
    pulled_t = dot(cot_t, iterate[...]).astype(bf16)
    right[v : v + one, :] = pulled_t
    right[v + one : v + two, :] = cot_t
    left[:, :one] = iterate[:, :one]
    left[:, one:two] = dot(iterate[...], iterate[:, :one]).astype(bf16)
    left[:, tail : tail + one] = x[:, :one]
    left[:, tail + one :] = square[:, :one]
    head[...] = 1.5 * cot_t.astype(f32) - 0.5 * dot(pulled_t, iterate[...])
    right[tail + one :, :] = (-2.0 * head[...]).astype(bf16)
    rows = jnp.concatenate([right[v : v + two, :], right[tail + one :, :]])
    for c in spans:
        onto_x = dot(rows, x[:, c])
        right[two:v, c] = onto_x[:two].astype(bf16)
        right[tail : tail + one, c] = onto_x[two:].astype(bf16)
        onto_square = dot(rows, square[:, c])
        right[:two, c] = onto_square[:two].astype(bf16)
        head_square[:, c] = onto_square[two:]
    w = left[:, :two]
    left[:, two:v] = dot(x[...], w).astype(bf16)
    left[:, v:tail] = dot(square[...], w).astype(bf16)

    for c in spans:
        cot = -0.5 * dot(left[:, :two], right[v : v + two, c])
        rest = 0.25 * dot(left[...], right[:, c])
        top = (cot[:one] + head[:, c]).astype(bf16).astype(f32)
        grad_t[:one, c] = (1.5 * top + rest[:one] + 0.25 * head_square[:, c]).astype(bf16)
        grad_t[one:, c] = (1.5 * cot[one:].astype(bf16).astype(f32) + rest[one:]).astype(bf16)

    departures = bulk(outs, staged, sent, False)
    for copy, ref, start in zip(departures, outs, starts_of(outs)):

        @pl.loop(start, start + ref.shape[0], unroll=16)
        def send(j):
            entry = entry_ref[1, j]
            block = grad_t[at(entry % edge, width), at(entry // edge, width)]
            staged[j] = kept(block, entry)

        copy.start()
    for copy in departures:
        copy.wait()


def adjoint_pieces(entry, keep, blocks, cot, counts, span=512):
    order, width = cot.shape
    arrays = len(blocks)
    anywhere = pl.BlockSpec(memory_space=pl.ANY)
    smem = pl.BlockSpec(memory_space=pltpu.SMEM)
    whole = pltpu.VMEM((order, order), jnp.bfloat16)
    strip = pltpu.VMEM((width, order), jnp.float32)
    return pl.pallas_call(
        functools.partial(adjoint_kernel, span, arrays),
        out_shape=[jax.ShapeDtypeStruct((count, width, width), jnp.bfloat16) for count in counts],
        in_specs=[smem, smem] + [anywhere] * arrays + [pl.BlockSpec(memory_space=pltpu.VMEM)],
        out_specs=[anywhere] * arrays,
        scratch_shapes=[whole] * 6
        + [strip] * 2
        + [pltpu.VMEM((sum(counts), width, width), jnp.bfloat16)]
        + [pltpu.SemaphoreType.DMA((arrays,))] * 2,
        compiler_params=pltpu.CompilerParams(vmem_limit_bytes=40 << 20),
        cost_estimate=pl.CostEstimate(flops=11_000_000_000, bytes_accessed=5 << 20, transcendentals=0),
    )(entry, keep, *blocks, cot)


def arrange(index, sources, counts, into_source_order=False, vmem_mb=16):
    given, total = sum(source.shape[0] for source in sources), sum(counts)

    def kernel(index_ref, *refs):
        ins, outs = refs[: len(sources)], refs[len(sources) : len(sources) + len(counts)]
        came, leaves, arrived, sent = refs[len(sources) + len(counts) :]
        arrivals = bulk(ins, came, arrived, True)
        departures = bulk(outs, leaves, sent, False)
        for copy in arrivals:
            copy.start()
        if into_source_order:
            for copy, ref, start in zip(arrivals, ins, starts_of(ins)):
                copy.wait()

                @pl.loop(start, start + ref.shape[0], unroll=16)
                def _(j):
                    leaves[index_ref[j]] = came[j]

            departures[0].start()
        else:
            for copy in arrivals:
                copy.wait()
            for copy, ref, start in zip(departures, outs, starts_of(outs)):

                @pl.loop(start, start + ref.shape[0], unroll=4 if ref.shape[0] % 4 == 0 else 2)
                def _(j):
                    leaves[j] = came[index_ref[j]]

                copy.start()
        for copy in departures:
            copy.wait()

    shape, dtype = sources[0].shape[1:], sources[0].dtype
    return pl.pallas_call(
        kernel,
        out_shape=[jax.ShapeDtypeStruct((count, *shape), dtype) for count in counts],
        in_specs=[pl.BlockSpec(memory_space=pltpu.SMEM)]
        + [pl.BlockSpec(memory_space=pl.ANY)] * len(sources),
        out_specs=[pl.BlockSpec(memory_space=pl.ANY)] * len(counts),
        scratch_shapes=[pltpu.VMEM((given, *shape), dtype), pltpu.VMEM((total, *shape), dtype)]
        + [pltpu.SemaphoreType.DMA((len(sources),)), pltpu.SemaphoreType.DMA((len(counts),))],
        compiler_params=pltpu.CompilerParams(vmem_limit_bytes=vmem_mb << 20),
        cost_estimate=pl.CostEstimate(flops=0, bytes_accessed=4 << 20, transcendentals=0),
    )(index, *sources)


AXES = ("x", "z", "core", "y")
SIZES = dict(x=4, z=8, core=2, y=4)
FIRST_LATE, LATE = 3, 3


def shift(blocks, axis, step):
    count = SIZES[axis]
    return lax.ppermute(blocks, axis, [(i, (i + step) % count) for i in range(count)])


def picked_sum(hits, values):
    return jnp.sum(jnp.where(hits, values, 0), axis=-1)


def tables(block_ids, slot_count):
    nx, nz, nk, ny = (SIZES[a] for a in AXES)
    mx, mz, mk, my = (lax.axis_index(a) for a in AXES)
    entries = block_ids.shape[1]
    room = entries // ny
    owners = block_ids // slot_count
    mine = owners == ((mx * nz + mz) * nk + mk) * ny + my
    asked = jnp.sum(jnp.where(mine, block_ids % slot_count, 0).reshape(nx * nz * nk, -1), axis=1)
    by_place = block_ids.reshape(nx, nz, nk, ny * entries)
    level = lax.dynamic_index_in_dim(by_place, mz, 1, keepdims=False)
    owner, slot = level // slot_count, level % slot_count
    row, oy = owner // ny, owner % ny
    ok, oz, ox = row % nk, row // nk % nz, row // (nk * nz)
    far = jnp.where((ox == mx) & (ok == mk) & (oy == my), (oz - mz) % nz, nz)
    slots = picked_sum(far[:, :, None, :] == jnp.arange(nz)[:, None], slot[:, :, None, :])
    slots = jnp.roll(jnp.roll(slots, -mx, axis=0), -mk, axis=1)

    def of_my_row(a):
        a = lax.dynamic_index_in_dim(a, mx, 0, keepdims=False)
        return lax.dynamic_index_in_dim(a, mk, 0, keepdims=False).reshape(ny, entries)

    row, oy, ok, oz, ox = (of_my_row(a) for a in (row, oy, ok, oz, ox))
    dk, dz, dx = (ok - mk) % nk, (oz - mz) % nz, (mx - ox) % nx
    late = (dz >= FIRST_LATE) & (dz < FIRST_LATE + LATE)
    early = nz - LATE
    group = jnp.where(late, LATE, early)
    within = jnp.where(dz < FIRST_LATE, dz, jnp.where(late, dz - FIRST_LATE, dz - LATE))
    stand = jnp.where(late, (nk + 1) * nx * early, 0) + within
    lane = jnp.where(dx == 0, 3, jnp.where(dx == 1, 0, jnp.where(dx == 3, 1, 2)))
    stand = stand + jnp.where(dk == 0, lane * nk, nk * nx + lane) * group
    here = oy == my
    rank = jnp.where(here, jnp.cumsum(here.astype(jnp.int32), axis=1) - 1, room)
    hits = rank[:, None, :] == jnp.arange(room)[:, None]
    ring = jnp.roll(picked_sum(hits, stand[:, None, :]), -my, axis=0)
    rows = jnp.roll(picked_sum(hits, row[:, None, :]), -my, axis=0)
    mine_y = lax.dynamic_index_in_dim(oy, my, 0, keepdims=False)
    there = (mine_y[None, :] - my) % ny == jnp.arange(ny)[:, None]
    rank = jnp.where(there, jnp.cumsum(there.astype(jnp.int32), axis=1) - 1, room)
    entry = picked_sum(rank[:, None, :] == jnp.arange(room)[:, None], jnp.arange(entries))
    return slots, asked, ring, rows, entry


def shards(h_blocks, block_ids, pattern, result_grad):
    nx, nz, nk, ny = (SIZES[a] for a in AXES)
    slot_count, width, _ = h_blocks.shape
    entries = block_ids.shape[1]
    room = entries // ny
    slots, asked, ring, rows, entry = tables(block_ids, slot_count)

    half = slot_count // 2
    up, down = [h_blocks], [h_blocks]
    for _ in range(nz // 2 - 1):
        up.append(shift(up[-1], "z", 1))
        down.append(shift(down[-1], "z", -1))
    up.append(shift(up[-1][:half], "z", 1))
    down.append(shift(down[-1][half:], "z", -1))
    early = [*down[:FIRST_LATE], up[2], up[1]]
    late = [down[3], up[4], down[4], up[3]]
    end = FIRST_LATE + LATE
    early_slots = jnp.concatenate([slots[:, :, :FIRST_LATE], slots[:, :, end:]], axis=2)

    def over_x_and_core(sources, wanted, vmem_mb):
        size = wanted.shape[2]
        wanted = wanted + slot_count * jnp.arange(size)
        order = jnp.concatenate([wanted[i].reshape(-1) for i in (1, 3, 2, 0)])
        ahead, behind, across, own = arrange(order, sources, [nk * size] * nx, vmem_mb=vmem_mb)
        came = [shift(ahead, "x", 1), shift(behind, "x", -1), shift(across, "x", 2), own]
        other = jnp.concatenate([part[size:] for part in came])
        return [*came, shift(other, "core", 1)]

    held = over_x_and_core(early, early_slots, 56)
    held = held + over_x_and_core(late, slots[:, :, FIRST_LATE:end], 16)

    routes = [(step, room // 1) for step in (1, -1, 2) for _ in range(1)]
    counts = [count for _, count in routes] + [room]

    def over_col(parts):
        return [shift(part, "y", step) for part, (step, _) in zip(parts, routes)] + [parts[-1]]

    order = jnp.concatenate([ring[i] for i in (1, 3, 2, 0)])
    blocks = over_col(arrange(order, held, counts))
    came = jnp.concatenate([entry[i] for i in (3, 1, 2, 0)])
    leaves = jnp.concatenate([entry[i] for i in (1, 3, 2, 0)])
    pieces = adjoint_pieces(
        jnp.stack([came, leaves]), pattern.reshape(-1), blocks, result_grad, counts
    )
    order = jnp.concatenate([rows[i] for i in (3, 1, 2, 0)])
    (held,) = arrange(order, over_col(pieces), [entries], into_source_order=True)

    held = lax.all_to_all(held, AXES[:3], split_axis=0, concat_axis=0, tiled=True)
    weights = (asked[None, :] == jnp.arange(slot_count)[:, None]).astype(jnp.bfloat16)
    return jnp.einsum("sr,rab->sba", weights, held, preferred_element_type=jnp.float32)


def solution(mesh):
    torus = Mesh(mesh.devices.reshape([SIZES[a] for a in AXES]), AXES)
    in_specs = (P(AXES, None, None), P(), P(AXES, None, None), P(AXES, None))
    return jax.shard_map(
        shards, mesh=torus, in_specs=in_specs, out_specs=P(AXES, None, None), check_vma=False
    )
```
